32 devices in a mesh: dev: 32 (over z, y, x, core).
Axes of the slice: x: 2, y: 2, z: 4, core: 2. Of those that a mesh axis runs over, the one named last changes fastest.
Arguments:
- residual: bfloat16 [4096, 2304], P('dev'), may hold values from -6 to 6
- queries: bfloat16 [4096, 2304], P('dev'), may hold values from -6 to 6
- new_kv: bfloat16 [4096, 4608], P('dev'), may hold values from -6 to 6
- page_kv: bfloat16 [256, 4608], P('dev'), may hold values from -6 to 6
- page_node: int32 [32], replicated, may hold values from 0 to 20
- leaf_parent: int32 [16], replicated, may hold values from 1 to 4
- request_leaf: int32 [32], P('dev'), may hold values from 5 to 20
- out_weight: bfloat16 [2304, 2304], replicated, may hold values from -0.125 to 0.125
- router_weight: bfloat16 [2304, 8], replicated, may hold values from -0.25 to 0.25
- routes: int32 [4096, 2], P('dev'), may hold values from 0 to 7, all different within a row; in each aligned block of 128 rows (0 to 127, 128 to 255, ...) at most 40 rows name the same one
- w_gate_up: bfloat16 [2, 46080, 2304], P(None, 'dev'), may hold values from -0.125 to 0.125
- w_down: bfloat16 [46080, 2304], P('dev'), may hold values from -0.078125 to 0.078125
Outputs:
- attended: bfloat16 [4096, 2304], P('dev')
- layer_out: bfloat16 [4096, 2304], P('dev')
The draws below stay inside these ranges and needn't reach their ends.
Inputs may be any that keep to these rules, and one draw needn't show every extreme that they name: `routes`: within the 128 rows of one device no expert is named by more than 40 rows, a bound that some block reaches.
All inputs are finite; a program needn't handle non-finite values.
Results may differ from the reference program's by a relative error of at most 0.012.
Values may be sent and summed in bfloat16 or wider, within the bound.
No kernel may reach another device: no remote copies, remote signals or barrier semaphores. Data moves between devices by JAX's collectives and lax.ppermute only.
A program may use at most 192 MiB of HBM per device.

```python
import math
import jax
import jax.numpy as jnp
import numpy as np
from jax import lax

D = 2304
HEADS = 36
HD = 64
EXPERTS = 8
TOP = 2
FF = 5760
TOK_DEV = 128
PAGE = 8
NB = 4
NL = 16
NODES = 21
REPL = 1
FSH = 1440
CAP = 40
TOKENS = 4096
PREFIX = 256
N_DEV = 32


def draw_queries(key, part):
    base_key = jax.random.fold_in(key, 11)
    values = jnp.clip(jax.random.normal(base_key, (TOKENS, D), jnp.float32), -6.0, 6.0)
    return values.astype(jnp.bfloat16)


def draw_page_kv(key, part):
    base_key = jax.random.fold_in(key, 23)
    values = jnp.clip(jax.random.normal(base_key, (PREFIX, 2 * D), jnp.float32), -6.0, 6.0)
    return values.astype(jnp.bfloat16)


def with_ends(drawn, key, low, largest):
    place = [jax.random.randint(jax.random.fold_in(key, axis), (), 0, length) for axis, length in enumerate(drawn.shape)]
    longest = drawn.shape.index(max(drawn.shape))
    neighbour = place[:longest] + [(place[longest] + 1) % drawn.shape[longest]] + place[longest + 1:]
    return drawn.at[tuple(place)].set(low).at[tuple(neighbour)].set(largest)


def steps_of(key, extent, pieces, least, top_value):
    loudness = 1.0
    for axis_at, shards_of in pieces:
        heights = jax.random.uniform(jax.random.fold_in(jax.random.fold_in(key, 6), axis_at), (shards_of,), jnp.float32, least / len(pieces), top_value / len(pieces))
        loudness = loudness * jnp.repeat(jnp.exp(heights), extent[axis_at] // shards_of).reshape((-1,) + (1,) * (len(extent) - 1 - axis_at))
    return loudness


def routed_block(key, own, number, rows, count, top, reach, lean):
    order = jax.random.permutation(key, count)
    crowded, usual = load_shares(count, rows * top, reach, lean, True), load_shares(count, rows * top, reach, lean, False)
    places = jnp.arange(count)

    def named(sizes, offset_by):
        used = int((sizes > 0).sum())
        fixed = max(1, used // 4)
        shifted = fixed + (places - fixed + offset_by * (used - fixed)) % max(1, count - fixed)
        return jnp.zeros((count,), jnp.int32).at[order[jnp.where(places < fixed, places, shifted)]].set(jnp.asarray(sizes, jnp.int32))

    sizes = jnp.where(number % 4 == 0, named(crowded, number // 4), named(usual, number - number // 4 - 1))
    mixed = jax.random.permutation(jax.random.fold_in(own, 3), count)
    source_of, taker = mixed[0:count // 2 * 2:2], mixed[1:count // 2 * 2:2]
    room = jnp.minimum(sizes[source_of] - 1, reach - sizes[taker]) // 2
    room = jnp.where((source_of == order[0]) | (taker == order[0]) | (sizes[taker] == 0), 0, jnp.maximum(room, 0))
    shifted = jax.random.randint(jax.random.fold_in(own, 4), (count // 2,), 0, 1 << 20) % (room + 1)
    sizes = sizes.at[source_of].add(-shifted).at[taker].add(shifted)
    labels = jnp.searchsorted(jnp.cumsum(sizes), jnp.arange(rows * top), side="right").astype(jnp.int32)
    listing = labels.reshape(top, rows).T
    listing = listing[jax.random.permutation(jax.random.fold_in(own, 1), rows)]
    offset_by = jax.random.randint(jax.random.fold_in(own, 2), (rows, 1), 0, top)
    return jnp.take_along_axis(listing, (jnp.arange(top)[None, :] + offset_by) % top, axis=1)


def load_shares(number_of, total, limit, lean, full):
    loads = [(1 << 20) // math.isqrt(rank ** lean) + 1 for rank in range(1, number_of + 1)]
    largest = limit if full else min(limit, max(-(-total // number_of), total * loads[0] // sum(loads)))
    least = 1 if total - largest >= number_of - 1 else 0
    holding, surplus = [largest] + [least] * (number_of - 1), total - largest - least * (number_of - 1)
    while surplus > 0:
        candidates = [i for i in range(1, number_of) if holding[i] < largest] or [i for i in range(1, number_of) if holding[i] < limit]
        pool, left = sum([loads[i] for i in candidates]), surplus
        for i in candidates:
            extra = min(limit - holding[i], max(1, left * loads[i] // pool), surplus)
            holding[i] = holding[i] + extra
            surplus = surplus - extra
    return np.array(holding)


def gaussian(own_key, dims, scale, most, split=(), held_as=jnp.bfloat16):
    array = scale * jax.random.normal(own_key, dims, jnp.float32)
    if split:
        array = array * steps_of(own_key, dims, split, -0.22, 0.18)
    return jnp.clip(array, -most, most).astype(held_as)


def setup_inputs(seed: int = 0) -> dict:
    arg_keys = jax.random.split(jax.random.key(seed), 13)
    residual = gaussian(arg_keys[0], (TOKENS, D), 1.0, 6.0, ((0, 32),))
    queries = draw_queries(jax.random.fold_in(arg_keys[12], 71), 0)
    new_kv = gaussian(arg_keys[2], (TOKENS, 2 * D), 1.0, 6.0, ((0, 32),))
    page_kv = draw_page_kv(jax.random.fold_in(arg_keys[12], 71), 0)
    page_node = with_ends(jax.random.randint(arg_keys[4], (N_DEV,), 0, NODES), jax.random.fold_in(arg_keys[4], 1), 0, NODES - 1).astype(jnp.int32)
    leaf_parent = with_ends(jax.random.randint(arg_keys[5], (NL,), 1, NB + 1), jax.random.fold_in(arg_keys[5], 1), 1, NB).astype(jnp.int32)
    request_leaf = with_ends(jax.random.randint(arg_keys[6], (N_DEV,), NB + 1, NODES), jax.random.fold_in(arg_keys[6], 1), NB + 1, NODES - 1).astype(jnp.int32)
    out_weight = gaussian(arg_keys[7], (D, D), D ** -0.5, 0.125)
    router_weight = gaussian(arg_keys[8], (D, EXPERTS), (D // 4) ** -0.5, 0.25)
    routes_keys = jax.random.split(jax.random.fold_in(arg_keys[9], 1), TOKENS // TOK_DEV)
    routes_turns = jax.random.permutation(jax.random.fold_in(arg_keys[9], 3), TOKENS // TOK_DEV)
    routes = jax.vmap(lambda own, number: routed_block(jax.random.fold_in(arg_keys[9], 2), own, number, TOK_DEV, EXPERTS, TOP, CAP, 2))(routes_keys, routes_turns).reshape((TOKENS, TOP))
    w_gate_up = gaussian(arg_keys[10], (2, N_DEV * FSH, D), D ** -0.5, 0.125, ((1, 32),))
    w_down = gaussian(arg_keys[11], (N_DEV * FSH, D), FF ** -0.5, 0.078125, ((0, 32),))
    return dict(residual=residual, queries=queries, new_kv=new_kv, page_kv=page_kv, page_node=page_node, leaf_parent=leaf_parent, request_leaf=request_leaf, out_weight=out_weight, router_weight=router_weight, routes=routes, w_gate_up=w_gate_up, w_down=w_down)


masked_fill = -1e+30
epsilon = 1e-05

def branch_of(leaf_node, leaf_parent):
    matches = jnp.arange(NL, dtype=jnp.int32) + NB + 1 == leaf_node
    return jnp.sum(jnp.where(matches, leaf_parent, 0)).astype(jnp.int32)

def attend(queries, new_kv, page_kv, page_node, leaf_parent, request_leaf):
    prefix_rows = page_kv.shape[0]
    position_node = jnp.repeat(page_node, PAGE)
    page_keys = page_kv[:, :D].astype(jnp.float32).reshape(prefix_rows, HEADS, HD)
    page_values = page_kv[:, D:].astype(jnp.float32).reshape(prefix_rows, HEADS, HD)
    causal = jnp.arange(TOK_DEV)[:, None] >= jnp.arange(TOK_DEV)[None, :]
    scale = HD ** (-0.5)

    def one_request(packed):
        query_rows, kv_rows, leaf_node = packed
        branch_node = branch_of(leaf_node, leaf_parent)
        visible = (position_node == 0) | (position_node == branch_node) | (position_node == leaf_node)
        all_keys = jnp.concatenate([page_keys, kv_rows[:, :D].astype(jnp.float32).reshape(TOK_DEV, HEADS, HD)], 0)
        all_values = jnp.concatenate([page_values, kv_rows[:, D:].astype(jnp.float32).reshape(TOK_DEV, HEADS, HD)], 0)
        full_mask = jnp.concatenate([jnp.broadcast_to(visible[None, :], (TOK_DEV, prefix_rows)), causal], 1)
        query_heads = query_rows.astype(jnp.float32).reshape(TOK_DEV, HEADS, HD)
        scores = jnp.einsum('qhd,khd->hqk', query_heads, all_keys) * scale
        scores = jnp.where(full_mask[None], scores, masked_fill)
        row_max = lax.optimization_barrier(jnp.max(scores, axis=-1, keepdims=True))
        probs = jnp.where(full_mask[None], jnp.exp(scores - row_max), 0.0)
        row_sum = lax.optimization_barrier(jnp.sum(probs, axis=-1))
        rounded = lax.optimization_barrier(probs.astype(jnp.bfloat16))
        mixed_heads = jnp.einsum('hqk,khd->hqd', rounded.astype(jnp.float32), all_values) / row_sum[..., None]
        return jnp.transpose(mixed_heads, (1, 0, 2)).reshape(TOK_DEV, D).astype(jnp.bfloat16)
    packed_all = (queries.reshape(N_DEV, TOK_DEV, D), new_kv.reshape(N_DEV, TOK_DEV, 2 * D), request_leaf)
    return lax.map(one_request, packed_all).reshape(TOKENS, D)

def reference(residual, queries, new_kv, page_kv, page_node, leaf_parent, request_leaf, out_weight, router_weight, routes, w_gate_up, w_down):
    attn_rows = attend(queries, new_kv, page_kv, page_node, leaf_parent, request_leaf)
    projected = jnp.dot(attn_rows, out_weight, preferred_element_type=jnp.float32)
    attended = (residual.astype(jnp.float32) + projected).astype(jnp.bfloat16)
    hidden_state = attended.astype(jnp.float32)
    normed = (hidden_state * lax.rsqrt(lax.optimization_barrier(jnp.mean(hidden_state * hidden_state, axis=-1, keepdims=True)) + epsilon)).astype(jnp.bfloat16)
    logits = jnp.dot(normed, router_weight, preferred_element_type=jnp.float32)
    expert_ids = jnp.arange(EXPERTS, dtype=jnp.int32)
    first_pick = routes[:, 0:1] == expert_ids
    second_pick = routes[:, 1:2] == expert_ids
    first_logit = lax.optimization_barrier(jnp.sum(jnp.where(first_pick, logits, 0.0), axis=1))
    second_logit = lax.optimization_barrier(jnp.sum(jnp.where(second_pick, logits, 0.0), axis=1))
    first_gate = 1.0 / (1.0 + jnp.exp(second_logit - first_logit))
    second_gate = 1.0 / (1.0 + jnp.exp(first_logit - second_logit))
    gate_share = jnp.where(first_pick, first_gate[:, None], 0.0) + jnp.where(second_pick, second_gate[:, None], 0.0)
    chosen = (first_pick | second_pick).astype(jnp.int32).reshape(N_DEV, TOK_DEV, EXPERTS)
    slot_rank = jnp.cumsum(chosen, axis=1) - 1
    slot_ids = jnp.arange(CAP, dtype=jnp.int32)
    slot_place = (chosen[..., None] == 1) & (slot_rank[..., None] == slot_ids)

    def fill_slots(packed):
        token_rows, place_dev = packed
        place_table = place_dev.reshape(TOK_DEV, EXPERTS * CAP).astype(jnp.bfloat16)
        return jnp.dot(place_table.T, token_rows, preferred_element_type=jnp.float32).astype(jnp.bfloat16).reshape(EXPERTS, CAP, D)
    slot_rows = lax.map(fill_slots, (normed.reshape(N_DEV, TOK_DEV, D), slot_place))
    gate_up_parts = w_gate_up.reshape(2, REPL, EXPERTS, 4, FSH, D)
    down_parts = w_down.reshape(REPL, EXPERTS, 4, FSH, D)
    contract = (((1,), (1,)), ((), ()))

    def run_expert(expert_id):
        expert_rows = lax.dynamic_index_in_dim(slot_rows, expert_id, 1, keepdims=False).reshape(N_DEV * CAP, D)
        gate_up_expert = lax.dynamic_index_in_dim(gate_up_parts, expert_id, 2, keepdims=False)
        down_expert = lax.dynamic_index_in_dim(down_parts, expert_id, 1, keepdims=False)
        summed = jnp.zeros((N_DEV * CAP, D), jnp.float32)
        for part_id in range(4):
            gate_rows = gate_up_expert[0, :, part_id].reshape(REPL * FSH, D)
            up_rows = gate_up_expert[1, :, part_id].reshape(REPL * FSH, D)
            down_rows = down_expert[:, part_id].reshape(REPL * FSH, D)
            gate_value = lax.dot_general(expert_rows, gate_rows, contract, preferred_element_type=jnp.float32)
            up_value = lax.dot_general(expert_rows, up_rows, contract, preferred_element_type=jnp.float32)
            hidden = (jax.nn.silu(gate_value) * up_value).astype(jnp.bfloat16)
            partial_out = lax.optimization_barrier(jnp.dot(hidden, down_rows, preferred_element_type=jnp.float32).astype(jnp.bfloat16))
            summed = summed + partial_out.astype(jnp.float32)
        return summed.reshape(N_DEV, CAP, D)
    expert_out = lax.map(run_expert, jnp.arange(EXPERTS, dtype=jnp.int32))
    combine_weight = slot_place.astype(jnp.float32) * gate_share.reshape(N_DEV, TOK_DEV, EXPERTS, 1)

    def combine(packed):
        weight_dev, out_dev = packed
        return jnp.einsum('tec,ecd->td', weight_dev, out_dev, precision=lax.Precision.HIGHEST)
    moe_out = lax.map(combine, (combine_weight, jnp.transpose(expert_out, (1, 0, 2, 3)))).reshape(TOKENS, D)
    layer_out = (hidden_state + moe_out).astype(jnp.bfloat16)
    return (attended, layer_out)
```

```python
import jax
import jax.numpy as jnp
from jax import lax
from jax.experimental import pallas as pl
from jax.experimental.pallas import tpu as pltpu
from jax.sharding import PartitionSpec as P

HD = 64
EXPERTS = 8
NB = 4
NL = 16
CAP = 40
BLOCK = 32

masked_fill = -1e30
epsilon = 1e-05
WHOLE = pl.BlockSpec(memory_space=pltpu.VMEM)
OVER_LAST = (((1,), (1,)), ((), ()))
OVER_FIRST = (((0,), (0,)), ((), ()))
GROUPS = ((0, 1), (2, 3), (4, 5), (6, 7))


def passed_along(shard, axis, by):
    length = lax.axis_size(axis)
    return lax.ppermute(shard, axis, [(i, (i + by) % length) for i in range(length)])


def swapped(shard, bits):
    length = lax.axis_size("dev")
    return lax.ppermute(shard, "dev", [(i, i ^ bits) for i in range(length)])


def gathered_pages(page_kv, width, replicas):
    column = jnp.concatenate([page_kv] + [swapped(page_kv, 8 * dz) for dz in (1, 2, 3)], axis=0)
    rows = column.shape[0]
    k_z, v_z = column[:, :width], column[:, width:]
    k_x = swapped(k_z, 2)
    v_y = swapped(v_z, 4)
    k_y = swapped(jnp.concatenate([k_z, k_x], axis=0), 4)
    v_x = swapped(jnp.concatenate([v_z, v_y], axis=0), 2)
    keys = jnp.concatenate([k_z, k_x, k_y], axis=0)
    values = jnp.concatenate([v_z, v_x[:rows], v_y, v_x[rows:]], axis=0)
    blocks = [(keys, values), (swapped(keys, 1), swapped(values, 1))]
    order = [c + y + x + z for c in (0, 1) for y in (0, 4) for x in (0, 2) for z in (0, 8, 16, 24)]
    for other in range(1, replicas):
        for pair in blocks[:2]:
            blocks.append(tuple(swapped(part, BLOCK * other) for part in pair))
    order = [BLOCK * other + place for other in range(replicas) for place in order]
    return [b[0] for b in blocks], [b[1] for b in blocks], order


def front(queries, new_kv, keys, values, bias, residual, out_weight, router_weight, routes, place_of):
    rows, width = queries.shape
    pairs = width // (2 * HD)
    blocks = len(keys)
    page = keys[0].shape[0]
    slots = EXPERTS * CAP
    routers = router_weight.shape[1]

    def body(*refs):
        q_ref, kv_ref = refs[:2]
        k_refs, v_refs = refs[2 : 2 + blocks], refs[2 + blocks : 2 + 2 * blocks]
        b_ref, res_ref, wo_ref, wr_ref, routes_ref, place_ref = refs[2 + 2 * blocks : 8 + 2 * blocks]
        att_ref, weight_ref = refs[8 + 2 * blocks : 10 + 2 * blocks]
        slot_refs = refs[10 + 2 * blocks : 18 + 2 * blocks]
        attn_ref = refs[-1]
        lane = lax.broadcasted_iota(jnp.int32, (rows, 2 * HD), 1)
        low = lane < HD
        row_at = lax.broadcasted_iota(jnp.int32, (2 * rows, rows), 0)
        row_at = jnp.where(row_at >= rows, row_at - rows, row_at)
        causal = row_at >= lax.broadcasted_iota(jnp.int32, (2 * rows, rows), 1)
        zero = jnp.zeros((rows, 2 * HD), jnp.bfloat16)
        for pair in range(pairs):
            cols = pl.ds(pair * 2 * HD, 2 * HD)
            q = q_ref[:, cols] * jnp.bfloat16(HD**-0.5)
            both = jnp.concatenate([jnp.where(low, q, zero), jnp.where(low, zero, q)], axis=0)
            own = lax.dot_general(
                both, kv_ref[:, cols], OVER_LAST, preferred_element_type=jnp.float32
            )
            scores = [jnp.where(causal, own, masked_fill)]
            for at in range(blocks):
                seen = lax.dot_general(
                    both, k_refs[at][:, cols], OVER_LAST, preferred_element_type=jnp.float32
                )
                scores.append(seen + b_ref[:, at * page : (at + 1) * page])
            top = jnp.max(scores[0], axis=1, keepdims=True)
            for s in scores[1:]:
                top = jnp.maximum(top, jnp.max(s, axis=1, keepdims=True))
            total = jnp.zeros((2 * rows, 1), jnp.float32)
            mixed = jnp.zeros((2 * rows, 2 * HD), jnp.float32)
            for at, s in enumerate(scores):
                probs = jnp.exp(s - top)
                total = total + jnp.sum(probs, axis=1, keepdims=True)
                value = (
                    kv_ref[:, pl.ds(width + pair * 2 * HD, 2 * HD)]
                    if at == 0
                    else v_refs[at - 1][:, cols]
                )
                mixed = mixed + jnp.dot(
                    probs.astype(jnp.bfloat16), value, preferred_element_type=jnp.float32
                )
            mixed = mixed / total
            attn_ref[:, cols] = jnp.where(low, mixed[:rows], mixed[rows:]).astype(jnp.bfloat16)
        projected = jnp.dot(attn_ref[...], wo_ref[...], preferred_element_type=jnp.float32)
        attended = (res_ref[...].astype(jnp.float32) + projected).astype(jnp.bfloat16)
        att_ref[...] = attended
        hidden = attended.astype(jnp.float32)
        normed = (
            hidden * lax.rsqrt(jnp.mean(hidden * hidden, axis=-1, keepdims=True) + epsilon)
        ).astype(jnp.bfloat16)
        column = lax.broadcasted_iota(jnp.int32, (rows, slots), 1)
        relative = jnp.zeros((rows, slots), jnp.int32)
        for step in range(1, EXPERTS):
            relative = relative + (column >= step * CAP).astype(jnp.int32)
        slot = (column - relative * CAP).astype(jnp.float32)
        expert = relative ^ place_ref[0]
        first = routes_ref[:, 0:1] == expert
        second = routes_ref[:, 1:2] == expert
        chosen = (first | second).astype(jnp.bfloat16)
        before = lax.broadcasted_iota(jnp.int32, (rows, rows), 0) > lax.broadcasted_iota(
            jnp.int32, (rows, rows), 1
        )
        rank = jnp.dot(before.astype(jnp.bfloat16), chosen, preferred_element_type=jnp.float32)
        here = rank == slot
        first, second = first & here, second & here
        table = (first | second).astype(jnp.bfloat16)
        slot_rows = lax.dot_general(
            table, normed, OVER_FIRST, preferred_element_type=jnp.float32
        ).astype(jnp.bfloat16)
        for r in range(EXPERTS):
            slot_refs[r][...] = slot_rows[r * CAP : (r + 1) * CAP]
        logits = jnp.dot(normed, wr_ref[...], preferred_element_type=jnp.float32)
        ids = lax.broadcasted_iota(jnp.int32, (rows, routers), 1)
        first_logit = jnp.sum(
            jnp.where(routes_ref[:, 0:1] == ids, logits, 0.0), axis=1, keepdims=True
        )
        second_logit = jnp.sum(
            jnp.where(routes_ref[:, 1:2] == ids, logits, 0.0), axis=1, keepdims=True
        )
        first_gate = 1.0 / (1.0 + jnp.exp(second_logit - first_logit))
        second_gate = 1.0 / (1.0 + jnp.exp(first_logit - second_logit))
        weight_ref[...] = jnp.where(first, first_gate, 0.0) + jnp.where(second, second_gate, 0.0)

    count = 8 + 2 * blocks
    specs = [WHOLE] * count
    specs[-1] = pl.BlockSpec(memory_space=pltpu.SMEM)
    return pl.pallas_call(
        body,
        in_specs=specs,
        out_specs=[WHOLE] * (2 + EXPERTS),
        out_shape=[
            jax.ShapeDtypeStruct((rows, width), jnp.bfloat16),
            jax.ShapeDtypeStruct((rows, slots), jnp.float32),
        ]
        + [jax.ShapeDtypeStruct((CAP, width), jnp.bfloat16)] * EXPERTS,
        scratch_shapes=[pltpu.VMEM((rows, width), jnp.bfloat16)],
        compiler_params=pltpu.CompilerParams(vmem_limit_bytes=24 << 20),
        cost_estimate=pl.CostEstimate(
            flops=2 * rows * width * (width + 4 * rows * (1 + blocks)),
            bytes_accessed=2 * width * width,
            transcendentals=pairs * 2 * rows * rows * (1 + blocks),
        ),
        name="front",
    )(queries, new_kv, *keys, *values, bias, residual, out_weight, router_weight, routes, place_of)


def expert_part(blocks, w_gate_up, w_down):
    rows, width = blocks[0].shape
    units = w_down.shape[0]
    cuts = 3
    step = units // cuts
    count = len(blocks)

    def body(*refs):
        in_refs, (up_ref, down_ref) = refs[:count], refs[count : count + 2]
        out_refs, (x_ref, total) = refs[count + 2 : 2 * count + 2], refs[2 * count + 2 :]
        for at in range(count):
            x_ref[pl.ds(at * rows, rows), :] = in_refs[at][...]
        for cut in range(cuts):
            part = pl.ds(cut * step, step)
            gate = lax.dot_general(
                x_ref[...], up_ref[0, part, :], OVER_LAST, preferred_element_type=jnp.float32
            )
            up = lax.dot_general(
                x_ref[...], up_ref[1, part, :], OVER_LAST, preferred_element_type=jnp.float32
            )
            hidden = (gate / (1.0 + jnp.exp(-gate)) * up).astype(jnp.bfloat16)
            out = jnp.dot(hidden, down_ref[part, :], preferred_element_type=jnp.float32)
            if cut == 0:
                total[...] = out
            elif cut < cuts - 1:
                total[...] += out
            else:
                done = (total[...] + out).astype(jnp.bfloat16)
                for at in range(count):
                    out_refs[at][...] = done[at * rows : (at + 1) * rows]

    return pl.pallas_call(
        body,
        in_specs=[WHOLE] * (count + 2),
        out_specs=[WHOLE] * count,
        out_shape=[jax.ShapeDtypeStruct((rows, width), jnp.bfloat16)] * count,
        scratch_shapes=[
            pltpu.VMEM((count * rows, width), jnp.bfloat16),
            pltpu.VMEM((count * rows, width), jnp.float32),
        ],
        compiler_params=pltpu.CompilerParams(
            vmem_limit_bytes=count * rows * width * 8 + (8 << 20)
        ),
        cost_estimate=pl.CostEstimate(
            flops=count * rows * width * units * 6,
            bytes_accessed=count * rows * width * 4,
            transcendentals=count * rows * units,
        ),
        name="expert_part",
    )(*blocks, w_gate_up, w_down)


def combined(attended, weight, pieces):
    rows, width = attended.shape

    def body(*refs):
        att_ref, weight_ref = refs[:2]
        piece_refs, out_ref, x_ref = refs[2 : 2 + EXPERTS], refs[-2], refs[-1]
        for r in range(EXPERTS):
            x_ref[pl.ds(r * CAP, CAP), :] = piece_refs[r][...]
        weight = weight_ref[...]
        high = weight.astype(jnp.bfloat16)
        low = (weight - high.astype(jnp.float32)).astype(jnp.bfloat16)
        moe = jnp.dot(high, x_ref[...], preferred_element_type=jnp.float32)
        moe = moe + jnp.dot(low, x_ref[...], preferred_element_type=jnp.float32)
        out_ref[...] = (att_ref[...].astype(jnp.float32) + moe).astype(jnp.bfloat16)

    return pl.pallas_call(
        body,
        in_specs=[WHOLE] * (2 + EXPERTS),
        out_specs=WHOLE,
        out_shape=jax.ShapeDtypeStruct((rows, width), jnp.bfloat16),
        scratch_shapes=[pltpu.VMEM((EXPERTS * CAP, width), jnp.bfloat16)],
        compiler_params=pltpu.CompilerParams(vmem_limit_bytes=16 << 20),
        name="combined",
    )(attended, weight, *pieces)


def experts(slots, w_gate_up, w_down):
    arrived = {0: slots[0]}
    for group in GROUPS:
        for r in group:
            if r:
                arrived[r] = swapped(slots[r], 4 * r)
    count = len(GROUPS)
    mine, beside, sums, kept, crossed = ([None] * count for _ in range(5))
    back = {}

    def bring(i):
        mine[i] = jnp.concatenate([arrived[r] for r in GROUPS[i]], axis=0)
        beside[i] = swapped(mine[i], 2)

    def send_home(i):
        rows = (kept[i] + crossed[i].astype(jnp.float32)).astype(jnp.bfloat16)
        for at, r in enumerate(GROUPS[i]):
            piece = rows[at * CAP : (at + 1) * CAP]
            back[r] = swapped(piece, 4 * r) if r else piece

    bring(0)
    bring(1)
    for i in range(count):
        blocks = [mine[i], beside[i], swapped(mine[i], 1), swapped(beside[i], 1)]
        if i:
            blocks = list(lax.optimization_barrier(tuple(blocks) + (sums[i - 1],)))
            crossed[i - 1] = swapped(blocks.pop(), 2)
        if i > 1:
            send_home(i - 2)
        out = expert_part(blocks, w_gate_up, w_down)
        other_mine, other_beside = swapped(out[2], 1), swapped(out[3], 1)
        kept[i] = out[0].astype(jnp.float32) + other_mine.astype(jnp.float32)
        sums[i] = (out[1].astype(jnp.float32) + other_beside.astype(jnp.float32)).astype(
            jnp.bfloat16
        )
        if i + 2 < count:
            bring(i + 2)
    crossed[count - 1] = swapped(sums[count - 1], 2)
    send_home(count - 2)
    send_home(count - 1)
    return [back[r] for r in range(EXPERTS)]


def per_device(
    residual,
    queries,
    new_kv,
    page_kv,
    page_node,
    leaf_parent,
    request_leaf,
    out_weight,
    router_weight,
    routes,
    w_gate_up,
    w_down,
):
    width = residual.shape[1]
    devices = lax.axis_size("dev")
    replicas = devices // BLOCK
    page_rows = page_kv.shape[0]
    gate_up_list = [w_gate_up]
    down_list = [w_down]
    for shift_step in range(1, replicas):
        arrived = passed_along((w_gate_up, w_down), "dev", BLOCK * shift_step)
        gate_up_list.append(arrived[0])
        down_list.append(arrived[1])
    if replicas > 1:
        w_gate_up = jnp.concatenate(gate_up_list, axis=1)
        w_down = jnp.concatenate(down_list, axis=0)
    me = lax.axis_index("dev")
    leaf_node = request_leaf[0]
    matches = jnp.arange(NL, dtype=jnp.int32) + NB + 1 == leaf_node
    branch_node = jnp.sum(jnp.where(matches, leaf_parent, 0))
    keys, values, order = gathered_pages(page_kv, width, replicas)
    owner = jnp.array(order, dtype=jnp.int32) ^ me
    owner = jnp.repeat(owner, page_rows)
    device_ids = jnp.arange(devices, dtype=jnp.int32)
    node_ids = jnp.sum(jnp.where(device_ids[:, None] == owner[None, :], page_node[:, None], 0), axis=0)
    visible = (node_ids == 0) | (node_ids == branch_node) | (node_ids == leaf_node)
    bias = jnp.where(visible, 0.0, masked_fill)[None, :]
    place_of = ((me % BLOCK) // 4).astype(jnp.int32).reshape(1)
    attended, weight, *slots = front(
        queries, new_kv, keys, values, bias, residual, out_weight, router_weight, routes, place_of
    )
    pieces = experts(slots, w_gate_up, w_down)
    return (attended, combined(attended, weight, pieces))


def solution(mesh):
    return jax.shard_map(
        per_device,
        mesh=mesh,
        in_specs=(
            P("dev", None),
            P("dev", None),
            P("dev", None),
            P("dev", None),
            P(),
            P(),
            P("dev"),
            P(),
            P(),
            P("dev", None),
            P(None, "dev", None),
            P("dev", None),
        ),
        out_specs=(P("dev", None), P("dev", None)),
        check_vma=False,
    )
```

```python
import jax
import jax.numpy as jnp
from jax import lax
from jax.experimental import pallas as pl
from jax.experimental.pallas import tpu as pltpu
from jax.sharding import PartitionSpec as P

HD = 64
EXPERTS = 8
NB = 4
NL = 16
CAP = 40
BLOCK = 32

masked_fill = -1e30
epsilon = 1e-05
WHOLE = pl.BlockSpec(memory_space=pltpu.VMEM)
OVER_LAST = (((1,), (1,)), ((), ()))
OVER_FIRST = (((0,), (0,)), ((), ()))


def passed_along(shard, axis, by):
    length = lax.axis_size(axis)
    return lax.ppermute(shard, axis, [(i, (i + by) % length) for i in range(length)])


def swapped(shard, bits):
    length = lax.axis_size("dev")
    return lax.ppermute(shard, "dev", [(i, i ^ bits) for i in range(length)])


def gathered_pages(page_kv, width, replicas, bias, tables):
    column = jnp.concatenate([page_kv] + [swapped(page_kv, 8 * dz) for dz in (1, 2, 3)], axis=0)
    rows = column.shape[0]
    column = after(column, bias)
    k_z, v_z = column[:, :width], column[:, width:]
    k_x = swapped(k_z, 2)
    v_y = swapped(v_z, 4)
    k_y = swapped(jnp.concatenate([k_z, k_x], axis=0), 4)
    v_x = swapped(jnp.concatenate([v_z, v_y], axis=0), 2)
    k_y, v_x = lax.optimization_barrier((k_y, v_x, *tables))[:2]
    keys = jnp.concatenate([k_z, k_x, k_y], axis=0)
    values = jnp.concatenate([v_z, v_x[:rows], v_y, v_x[rows:]], axis=0)
    blocks = [(keys, values), (swapped(keys, 1), swapped(values, 1))]
    for other in range(1, replicas):
        for pair in blocks[:2]:
            blocks.append(tuple(swapped(part, BLOCK * other) for part in pair))
    return [b[0] for b in blocks], [b[1] for b in blocks]


def slot_tables(routes, place_of, *ahead):
    rows = routes.shape[1]
    slots = EXPERTS * CAP

    def body(routes_ref, place_ref, *refs):
        marks_ref, picks_ref = refs[len(ahead) :]
        picks = [
            jnp.transpose(
                jnp.broadcast_to(routes_ref[at : at + 1, :].astype(jnp.float32), (rows, rows))
            )[:, 0:1].astype(jnp.int32)
            for at in (0, 1)
        ]
        column = lax.broadcasted_iota(jnp.int32, (rows, slots), 1)
        relative = jnp.zeros((rows, slots), jnp.int32)
        for step in range(1, EXPERTS):
            relative = relative + (column >= step * CAP).astype(jnp.int32)
        slot = (column - relative * CAP).astype(jnp.float32)
        expert = relative ^ place_ref[0]
        first = picks[0] == expert
        second = picks[1] == expert
        chosen = (first | second).astype(jnp.bfloat16)
        before = lax.broadcasted_iota(jnp.int32, (rows, rows), 0) > lax.broadcasted_iota(
            jnp.int32, (rows, rows), 1
        )
        rank = jnp.dot(before.astype(jnp.bfloat16), chosen, preferred_element_type=jnp.float32)
        here = rank == slot
        first, second = first & here, second & here
        ids = lax.broadcasted_iota(jnp.int32, (rows, EXPERTS), 1)
        for at, mark in enumerate((first, second)):
            marks_ref[at] = mark.astype(jnp.bfloat16)
            picks_ref[at] = (picks[at] == ids).astype(jnp.float32)

    return pl.pallas_call(
        body,
        in_specs=[WHOLE, pl.BlockSpec(memory_space=pltpu.SMEM)] + [WHOLE] * len(ahead),
        out_specs=[WHOLE] * 2,
        out_shape=[
            jax.ShapeDtypeStruct((2, rows, slots), jnp.bfloat16),
            jax.ShapeDtypeStruct((2, rows, EXPERTS), jnp.float32),
        ],
        compiler_params=pltpu.CompilerParams(vmem_limit_bytes=8 << 20),
        cost_estimate=pl.CostEstimate(flops=1, bytes_accessed=1 << 20, transcendentals=1),
        name="slot_tables",
    )(routes, place_of, *ahead)


def front(queries, new_kv, keys, values, bias, residual, out_weight, router_weight, marks, picks):
    rows, width = queries.shape
    pairs = width // (2 * HD)
    blocks = len(keys)
    page = keys[0].shape[0]
    slots = EXPERTS * CAP

    def body(*refs):
        q_ref, kv_ref = refs[:2]
        k_refs, v_refs = refs[2 : 2 + blocks], refs[2 + blocks : 2 + 2 * blocks]
        b_ref, res_ref, wo_ref, wr_ref, marks_ref, picks_ref = refs[2 + 2 * blocks : 8 + 2 * blocks]
        att_ref, weight_ref = refs[8 + 2 * blocks : 10 + 2 * blocks]
        slot_refs = refs[10 + 2 * blocks : 18 + 2 * blocks]
        attn_ref = refs[-1]
        lane = lax.broadcasted_iota(jnp.int32, (rows, 2 * HD), 1)
        low = lane < HD
        row_at = lax.broadcasted_iota(jnp.int32, (2 * rows, rows), 0)
        row_at = jnp.where(row_at >= rows, row_at - rows, row_at)
        causal = row_at >= lax.broadcasted_iota(jnp.int32, (2 * rows, rows), 1)
        zero = jnp.zeros((rows, 2 * HD), jnp.bfloat16)
        for pair in range(pairs):
            cols = pl.ds(pair * 2 * HD, 2 * HD)
            q = q_ref[:, cols] * jnp.bfloat16(HD**-0.5)
            both = jnp.concatenate([jnp.where(low, q, zero), jnp.where(low, zero, q)], axis=0)
            own = lax.dot_general(
                both, kv_ref[:, cols], OVER_LAST, preferred_element_type=jnp.float32
            )
            scores = [jnp.where(causal, own, masked_fill)]
            for at in range(blocks):
                seen = lax.dot_general(
                    both, k_refs[at][:, cols], OVER_LAST, preferred_element_type=jnp.float32
                )
                scores.append(seen + b_ref[:, at * page : (at + 1) * page])
            top = jnp.max(scores[0], axis=1, keepdims=True)
            for s in scores[1:]:
                top = jnp.maximum(top, jnp.max(s, axis=1, keepdims=True))
            total = jnp.zeros((2 * rows, 1), jnp.float32)
            mixed = jnp.zeros((2 * rows, 2 * HD), jnp.float32)
            for at, s in enumerate(scores):
                probs = jnp.exp(s - top)
                total = total + jnp.sum(probs, axis=1, keepdims=True)
                value = (
                    kv_ref[:, pl.ds(width + pair * 2 * HD, 2 * HD)]
                    if at == 0
                    else v_refs[at - 1][:, cols]
                )
                mixed = mixed + jnp.dot(
                    probs.astype(jnp.bfloat16), value, preferred_element_type=jnp.float32
                )
            mixed = mixed / total
            attn_ref[:, cols] = jnp.where(low, mixed[:rows], mixed[rows:]).astype(jnp.bfloat16)
        projected = jnp.dot(attn_ref[...], wo_ref[...], preferred_element_type=jnp.float32)
        attended = (res_ref[...].astype(jnp.float32) + projected).astype(jnp.bfloat16)
        att_ref[...] = attended
        hidden = attended.astype(jnp.float32)
        normed = (
            hidden * lax.rsqrt(jnp.mean(hidden * hidden, axis=-1, keepdims=True) + epsilon)
        ).astype(jnp.bfloat16)
        first, second = marks_ref[0], marks_ref[1]
        table = first + second
        slot_rows = lax.dot_general(
            table, normed, OVER_FIRST, preferred_element_type=jnp.float32
        ).astype(jnp.bfloat16)
        for r in range(EXPERTS):
            slot_refs[r][...] = slot_rows[r * CAP : (r + 1) * CAP]
        logits = lax.dot_general(
            normed, wr_ref[...], OVER_LAST, preferred_element_type=jnp.float32
        )
        first_logit = jnp.sum(
            jnp.where(picks_ref[0] > 0, logits, 0.0), axis=1, keepdims=True
        )
        second_logit = jnp.sum(
            jnp.where(picks_ref[1] > 0, logits, 0.0), axis=1, keepdims=True
        )
        first_gate = 1.0 / (1.0 + jnp.exp(second_logit - first_logit))
        second_gate = 1.0 / (1.0 + jnp.exp(first_logit - second_logit))
        weight_ref[...] = jnp.where(first > 0, first_gate, 0.0) + jnp.where(
            second > 0, second_gate, 0.0
        )

    count = 8 + 2 * blocks
    return pl.pallas_call(
        body,
        in_specs=[WHOLE] * count,
        out_specs=[WHOLE] * (2 + EXPERTS),
        out_shape=[
            jax.ShapeDtypeStruct((rows, width), jnp.bfloat16),
            jax.ShapeDtypeStruct((rows, slots), jnp.float32),
        ]
        + [jax.ShapeDtypeStruct((CAP, width), jnp.bfloat16)] * EXPERTS,
        scratch_shapes=[
            pltpu.VMEM((rows, width), jnp.bfloat16),
        ],
        compiler_params=pltpu.CompilerParams(vmem_limit_bytes=12 << 20),
        cost_estimate=pl.CostEstimate(
            flops=2 * rows * width * (width + 4 * rows * (1 + blocks)),
            bytes_accessed=6 * width * width,
            transcendentals=pairs * 2 * rows * rows * (1 + blocks),
        ),
        name="front",
    )(queries, new_kv, *keys, *values, bias, residual, out_weight, router_weight, marks, picks)


def expert_part(blocks, w_gate_up, w_down):
    rows, width = blocks[0].shape
    units = w_down.shape[0]
    cuts = 3
    step = units // cuts
    count = len(blocks)

    def body(*refs):
        in_refs, (up_ref, down_ref) = refs[:count], refs[count : count + 2]
        out_refs, (x_ref, total) = refs[count + 2 : 2 * count + 2], refs[2 * count + 2 :]
        for at in range(count):
            x_ref[pl.ds(at * rows, rows), :] = in_refs[at][...]
        for cut in range(cuts):
            part = pl.ds(cut * step, step)
            gate = lax.dot_general(
                x_ref[...], up_ref[0, part, :], OVER_LAST, preferred_element_type=jnp.float32
            )
            up = lax.dot_general(
                x_ref[...], up_ref[1, part, :], OVER_LAST, preferred_element_type=jnp.float32
            )
            hidden = (gate / (1.0 + jnp.exp(-gate)) * up).astype(jnp.bfloat16)
            out = jnp.dot(hidden, down_ref[part, :], preferred_element_type=jnp.float32)
            if cut == 0:
                total[...] = out
            elif cut < cuts - 1:
                total[...] += out
            else:
                done = (total[...] + out).astype(jnp.bfloat16)
                for at in range(count):
                    out_refs[at][...] = done[at * rows : (at + 1) * rows]

    return pl.pallas_call(
        body,
        in_specs=[WHOLE] * (count + 2),
        out_specs=[WHOLE] * count,
        out_shape=[jax.ShapeDtypeStruct((rows, width), jnp.bfloat16)] * count,
        scratch_shapes=[
            pltpu.VMEM((count * rows, width), jnp.bfloat16),
            pltpu.VMEM((count * rows, width), jnp.float32),
        ],
        compiler_params=pltpu.CompilerParams(
            vmem_limit_bytes=count * rows * width * 8 + (8 << 20)
        ),
        cost_estimate=pl.CostEstimate(
            flops=count * rows * width * units * 6,
            bytes_accessed=count * rows * width * 4,
            transcendentals=count * rows * units,
        ),
        name="expert_part",
    )(*blocks, w_gate_up, w_down)


def combined(attended, weight, pieces):
    rows, width = attended.shape

    def body(*refs):
        att_ref, weight_ref = refs[:2]
        piece_refs, out_ref, x_ref = refs[2 : 2 + EXPERTS], refs[-2], refs[-1]
        for r in range(EXPERTS):
            x_ref[pl.ds(r * CAP, CAP), :] = piece_refs[r][...]
        weight = weight_ref[...]
        high = weight.astype(jnp.bfloat16)
        low = (weight - high.astype(jnp.float32)).astype(jnp.bfloat16)
        moe = jnp.dot(high, x_ref[...], preferred_element_type=jnp.float32)
        moe = moe + jnp.dot(low, x_ref[...], preferred_element_type=jnp.float32)
        out_ref[...] = (att_ref[...].astype(jnp.float32) + moe).astype(jnp.bfloat16)

    return pl.pallas_call(
        body,
        in_specs=[WHOLE] * (2 + EXPERTS),
        out_specs=WHOLE,
        out_shape=jax.ShapeDtypeStruct((rows, width), jnp.bfloat16),
        scratch_shapes=[pltpu.VMEM((EXPERTS * CAP, width), jnp.bfloat16)],
        compiler_params=pltpu.CompilerParams(vmem_limit_bytes=16 << 20),
        name="combined",
    )(attended, weight, *pieces)


def after(value, *events):
    return lax.optimization_barrier((value,) + events)[0]


def experts(slots, w_gate_up, w_down):
    def added(first, *others):
        total = first.astype(jnp.float32)
        for other in others:
            total = total + other.astype(jnp.float32)
        return total.astype(jnp.bfloat16)

    together = lax.optimization_barrier
    join = lambda *pieces: jnp.concatenate(pieces, axis=0)

    def part(mine, beside, before=(), behind=()):
        blocks = (mine, beside, swapped(mine, 1), swapped(beside, 1))
        if before:
            blocks = together((*blocks, *before))[:4]
        out = expert_part(blocks, w_gate_up, w_down)
        if behind:
            out = together((*out, *behind))[:4]
        return (out[0], swapped(out[2], 1)), added(out[1], swapped(out[3], 1))

    def home(rows, group):
        return [
            swapped(rows[at * CAP : (at + 1) * CAP], 4 * r) if r else rows[:CAP]
            for at, r in enumerate(group)
        ]

    z_1, x_0 = swapped(slots[1], 4), swapped(slots[0], 2)
    z_2, z_3 = swapped(slots[2], 8), swapped(slots[3], 12)
    z_4, z_5 = swapped(slots[4], 16), swapped(slots[5], 20)
    z_6 = swapped(after(slots[6], z_2, z_3), 24)
    z_7 = swapped(after(slots[7], z_2, z_3), 28)
    mine_a, mine_b = join(slots[0], z_1), join(z_2, z_3)
    beside_a, beside_b = join(x_0, swapped(z_1, 2)), swapped(mine_b, 2)
    own_a, sum_a = part(mine_a, beside_a)
    mine_c = join(after(z_4, own_a[0]), after(z_5, own_a[0]))
    beside_c = swapped(mine_c, 2)
    ret_a = swapped(sum_a, 2)
    own_b, sum_b = part(mine_b, beside_b, before=(sum_a,), behind=(beside_c,))
    mine_d = join(after(z_6, own_b[0]), after(z_7, own_b[0]))
    beside_d = swapped(mine_d, 2)
    own_c, sum_c = part(mine_c, beside_c, before=(sum_a, sum_b), behind=(beside_d, ret_a))
    ret_c = swapped(sum_c, 2)
    own_d, sum_d = part(mine_d, beside_d, before=(sum_c,), behind=(ret_c,))
    ret_d = swapped(sum_d, 2)
    home_a = home(added(*own_a, ret_a), (0, 1))
    home_c = home(added(*own_c, ret_c), (4, 5))
    ret_b = swapped(after(sum_b, ret_d), 2)
    home_d = home(added(*own_d, ret_d), (6, 7))
    home_b = home(added(*own_b, ret_b), (2, 3))
    return home_a + home_b + home_c + home_d


def per_device(
    residual,
    queries,
    new_kv,
    page_kv,
    page_node,
    leaf_parent,
    request_leaf,
    out_weight,
    router_weight,
    routes,
    w_gate_up,
    w_down,
):
    width = residual.shape[1]
    devices = lax.axis_size("dev")
    replicas = devices // BLOCK
    page_rows = page_kv.shape[0]
    gate_up_list = [w_gate_up]
    down_list = [w_down]
    for shift_step in range(1, replicas):
        arrived = passed_along((w_gate_up, w_down), "dev", BLOCK * shift_step)
        gate_up_list.append(arrived[0])
        down_list.append(arrived[1])
    if replicas > 1:
        w_gate_up = jnp.concatenate(gate_up_list, axis=1)
        w_down = jnp.concatenate(down_list, axis=0)
    me = lax.axis_index("dev")
    leaf_node = request_leaf[0]
    matches = jnp.arange(NL, dtype=jnp.int32) + NB + 1 == leaf_node
    branch_node = jnp.sum(jnp.where(matches, leaf_parent, 0))
    order = [c + y + x + z for c in (0, 1) for y in (0, 4) for x in (0, 2) for z in (0, 8, 16, 24)]
    order = [BLOCK * other + place for other in range(replicas) for place in order]
    owner = jnp.array(order, dtype=jnp.int32) ^ me
    owner = jnp.repeat(owner, page_rows)
    device_ids = jnp.arange(devices, dtype=jnp.int32)
    node_ids = jnp.sum(jnp.where(device_ids[:, None] == owner[None, :], page_node[:, None], 0), axis=0)
    visible = (node_ids == 0) | (node_ids == branch_node) | (node_ids == leaf_node)
    bias = jnp.where(visible, 0.0, masked_fill)[None, :]
    place_of = ((me % BLOCK) // 4).astype(jnp.int32).reshape(1)
    marks, picks = slot_tables(routes.T, place_of, out_weight)
    keys, values = gathered_pages(page_kv, width, replicas, bias, (marks, picks))
    attended, weight, *slots = front(
        queries, new_kv, keys, values, bias, residual, out_weight, router_weight.T, marks, picks
    )
    pieces = experts(slots, w_gate_up, w_down)
    return (attended, combined(attended, weight, pieces))


def solution(mesh):
    return jax.shard_map(
        per_device,
        mesh=mesh,
        in_specs=(
            P("dev", None),
            P("dev", None),
            P("dev", None),
            P("dev", None),
            P(),
            P(),
            P("dev"),
            P(),
            P(),
            P("dev", None),
            P(None, "dev", None),
            P("dev", None),
        ),
        out_specs=(P("dev", None), P("dev", None)),
        check_vma=False,
    )
```

```python
import jax
import jax.numpy as jnp
from jax import lax
from jax.experimental import pallas as pl
from jax.experimental.pallas import tpu as pltpu
from jax.sharding import PartitionSpec as P

HD = 64
EXPERTS = 8
NB = 4
NL = 16
CAP = 40
BLOCK = 32

masked_fill = -1e30
epsilon = 1e-05
WHOLE = pl.BlockSpec(memory_space=pltpu.VMEM)
OVER_LAST = (((1,), (1,)), ((), ()))
OVER_FIRST = (((0,), (0,)), ((), ()))


def passed_along(shard, axis, by):
    length = lax.axis_size(axis)
    return lax.ppermute(shard, axis, [(i, (i + by) % length) for i in range(length)])


def swapped(shard, bits):
    length = lax.axis_size("dev")
    return lax.ppermute(shard, "dev", [(i, i ^ bits) for i in range(length)])


def gathered_pages(page_kv, width, replicas, bias, tables):
    column = jnp.concatenate([page_kv] + [swapped(page_kv, 8 * dz) for dz in (1, 2, 3)], axis=0)
    rows = column.shape[0]
    column = after(column, bias)
    k_z, v_z = column[:, :width], column[:, width:]
    k_x = swapped(k_z, 2)
    v_y = swapped(v_z, 4)
    k_y = swapped(jnp.concatenate([k_z, k_x], axis=0), 4)
    v_x = swapped(jnp.concatenate([v_z, v_y], axis=0), 2)
    k_y, v_x = lax.optimization_barrier((k_y, v_x, *tables))[:2]
    keys = jnp.concatenate([k_z, k_x, k_y], axis=0)
    values = jnp.concatenate([v_z, v_x[:rows], v_y, v_x[rows:]], axis=0)
    blocks = [(keys, values), (swapped(keys, 1), swapped(values, 1))]
    for other in range(1, replicas):
        for pair in blocks[:2]:
            blocks.append(tuple(swapped(part, BLOCK * other) for part in pair))
    return [b[0] for b in blocks], [b[1] for b in blocks]


def slot_tables(routes, place_of, *ahead):
    rows = routes.shape[1]
    slots = EXPERTS * CAP

    def body(routes_ref, place_ref, *refs):
        marks_ref, picks_ref = refs[len(ahead) :]
        picks = [
            jnp.transpose(
                jnp.broadcast_to(routes_ref[at : at + 1, :].astype(jnp.float32), (rows, rows))
            )[:, 0:1].astype(jnp.int32)
            for at in (0, 1)
        ]
        column = lax.broadcasted_iota(jnp.int32, (rows, slots), 1)
        relative = jnp.zeros((rows, slots), jnp.int32)
        for step in range(1, EXPERTS):
            relative = relative + (column >= step * CAP).astype(jnp.int32)
        slot = (column - relative * CAP).astype(jnp.float32)
        expert = relative ^ place_ref[0]
        first = picks[0] == expert
        second = picks[1] == expert
        chosen = (first | second).astype(jnp.bfloat16)
        before = lax.broadcasted_iota(jnp.int32, (rows, rows), 0) > lax.broadcasted_iota(
            jnp.int32, (rows, rows), 1
        )
        rank = jnp.dot(before.astype(jnp.bfloat16), chosen, preferred_element_type=jnp.float32)
        here = rank == slot
        first, second = first & here, second & here
        ids = lax.broadcasted_iota(jnp.int32, (rows, EXPERTS), 1)
        for at, mark in enumerate((first, second)):
            marks_ref[at] = mark.astype(jnp.bfloat16)
            picks_ref[at] = (picks[at] == ids).astype(jnp.float32)

    return pl.pallas_call(
        body,
        in_specs=[WHOLE, pl.BlockSpec(memory_space=pltpu.SMEM)] + [WHOLE] * len(ahead),
        out_specs=[WHOLE] * 2,
        out_shape=[
            jax.ShapeDtypeStruct((2, rows, slots), jnp.bfloat16),
            jax.ShapeDtypeStruct((2, rows, EXPERTS), jnp.float32),
        ],
        compiler_params=pltpu.CompilerParams(vmem_limit_bytes=8 << 20),
        cost_estimate=pl.CostEstimate(flops=1, bytes_accessed=1 << 20, transcendentals=1),
        name="slot_tables",
    )(routes, place_of, *ahead)


def front(queries, new_kv, keys, values, bias, residual, out_weight, router_weight, marks, picks):
    rows, width = queries.shape
    pairs = width // (2 * HD)
    blocks = len(keys)
    page = keys[0].shape[0]
    slots = EXPERTS * CAP

    def body(*refs):
        q_ref, kv_ref = refs[:2]
        k_refs, v_refs = refs[2 : 2 + blocks], refs[2 + blocks : 2 + 2 * blocks]
        b_ref, res_ref, wo_ref, wr_ref, marks_ref, picks_ref = refs[2 + 2 * blocks : 8 + 2 * blocks]
        att_ref, weight_ref = refs[8 + 2 * blocks : 10 + 2 * blocks]
        slot_refs = refs[10 + 2 * blocks : 18 + 2 * blocks]
        attn_ref = refs[-1]
        lane = lax.broadcasted_iota(jnp.int32, (rows, 2 * HD), 1)
        low = lane < HD
        row_at = lax.broadcasted_iota(jnp.int32, (2 * rows, rows), 0)
        row_at = jnp.where(row_at >= rows, row_at - rows, row_at)
        causal = row_at >= lax.broadcasted_iota(jnp.int32, (2 * rows, rows), 1)
        zero = jnp.zeros((rows, 2 * HD), jnp.bfloat16)
        for pair in range(pairs):
            cols = pl.ds(pair * 2 * HD, 2 * HD)
            q = q_ref[:, cols] * jnp.bfloat16(HD**-0.5)
            both = jnp.concatenate([jnp.where(low, q, zero), jnp.where(low, zero, q)], axis=0)
            own = lax.dot_general(
                both, kv_ref[:, cols], OVER_LAST, preferred_element_type=jnp.float32
            )
            scores = [jnp.where(causal, own, masked_fill)]
            for at in range(blocks):
                seen = lax.dot_general(
                    both, k_refs[at][:, cols], OVER_LAST, preferred_element_type=jnp.float32
                )
                scores.append(seen + b_ref[:, at * page : (at + 1) * page])
            top = jnp.max(scores[0], axis=1, keepdims=True)
            for s in scores[1:]:
                top = jnp.maximum(top, jnp.max(s, axis=1, keepdims=True))
            total = jnp.zeros((2 * rows, 1), jnp.float32)
            mixed = jnp.zeros((2 * rows, 2 * HD), jnp.float32)
            for at, s in enumerate(scores):
                probs = jnp.exp(s - top)
                total = total + jnp.sum(probs, axis=1, keepdims=True)
                value = (
                    kv_ref[:, pl.ds(width + pair * 2 * HD, 2 * HD)]
                    if at == 0
                    else v_refs[at - 1][:, cols]
                )
                mixed = mixed + jnp.dot(
                    probs.astype(jnp.bfloat16), value, preferred_element_type=jnp.float32
                )
            mixed = mixed / total
            attn_ref[:, cols] = jnp.where(low, mixed[:rows], mixed[rows:]).astype(jnp.bfloat16)
        projected = jnp.dot(attn_ref[...], wo_ref[...], preferred_element_type=jnp.float32)
        attended = (res_ref[...].astype(jnp.float32) + projected).astype(jnp.bfloat16)
        att_ref[...] = attended
        hidden = attended.astype(jnp.float32)
        normed = (
            hidden * lax.rsqrt(jnp.mean(hidden * hidden, axis=-1, keepdims=True) + epsilon)
        ).astype(jnp.bfloat16)
        first, second = marks_ref[0], marks_ref[1]
        table = first + second
        slot_rows = lax.dot_general(
            table, normed, OVER_FIRST, preferred_element_type=jnp.float32
        ).astype(jnp.bfloat16)
        for r in range(EXPERTS):
            slot_refs[r][...] = slot_rows[r * CAP : (r + 1) * CAP]
        logits = lax.dot_general(
            normed, wr_ref[...], OVER_LAST, preferred_element_type=jnp.float32
        )
        first_logit = jnp.sum(
            jnp.where(picks_ref[0] > 0, logits, 0.0), axis=1, keepdims=True
        )
        second_logit = jnp.sum(
            jnp.where(picks_ref[1] > 0, logits, 0.0), axis=1, keepdims=True
        )
        first_gate = 1.0 / (1.0 + jnp.exp(second_logit - first_logit))
        second_gate = 1.0 / (1.0 + jnp.exp(first_logit - second_logit))
        weight_ref[...] = jnp.where(first > 0, first_gate, 0.0) + jnp.where(
            second > 0, second_gate, 0.0
        )

    count = 8 + 2 * blocks
    return pl.pallas_call(
        body,
        in_specs=[WHOLE] * count,
        out_specs=[WHOLE] * (2 + EXPERTS),
        out_shape=[
            jax.ShapeDtypeStruct((rows, width), jnp.bfloat16),
            jax.ShapeDtypeStruct((rows, slots), jnp.float32),
        ]
        + [jax.ShapeDtypeStruct((CAP, width), jnp.bfloat16)] * EXPERTS,
        scratch_shapes=[
            pltpu.VMEM((rows, width), jnp.bfloat16),
        ],
        compiler_params=pltpu.CompilerParams(vmem_limit_bytes=12 << 20),
        cost_estimate=pl.CostEstimate(
            flops=2 * rows * width * (width + 4 * rows * (1 + blocks)),
            bytes_accessed=6 * width * width,
            transcendentals=pairs * 2 * rows * rows * (1 + blocks),
        ),
        name="front",
    )(queries, new_kv, *keys, *values, bias, residual, out_weight, router_weight, marks, picks)


def expert_part(blocks, w_gate_up, w_down):
    rows, width = blocks[0].shape
    units = w_down.shape[0]
    cuts = 3
    step, columns = units // cuts, width // cuts
    count = len(blocks)

    def body(*refs):
        in_refs, (up_ref, down_ref) = refs[:count], refs[count : count + 2]
        out_refs, (x_ref, hidden_ref) = refs[count + 2 : 2 * count + 2], refs[2 * count + 2 :]
        for at in range(count):
            x_ref[pl.ds(at * rows, rows), :] = in_refs[at][...]

        @pl.loop(0, cuts)
        def _(cut):
            part = pl.ds(pl.multiple_of(cut * step, 16), step)
            gate = lax.dot_general(
                x_ref[...], up_ref[0, part, :], OVER_LAST, preferred_element_type=jnp.float32
            )
            up = lax.dot_general(
                x_ref[...], up_ref[1, part, :], OVER_LAST, preferred_element_type=jnp.float32
            )
            hidden_ref[cut] = (gate / (1.0 + jnp.exp(-gate)) * up).astype(jnp.bfloat16)

        @pl.loop(0, cuts)
        def _(cut):
            cols = pl.ds(pl.multiple_of(cut * columns, 128), columns)
            out = jnp.dot(
                hidden_ref[0], down_ref[:step, cols], preferred_element_type=jnp.float32
            )
            for at in range(1, cuts):
                out = out + jnp.dot(
                    hidden_ref[at],
                    down_ref[at * step : (at + 1) * step, cols],
                    preferred_element_type=jnp.float32,
                )
            out = out.astype(jnp.bfloat16)
            for at in range(count):
                out_refs[at][:, cols] = out[at * rows : (at + 1) * rows]

    return pl.pallas_call(
        body,
        in_specs=[WHOLE] * (count + 2),
        out_specs=[WHOLE] * count,
        out_shape=[jax.ShapeDtypeStruct((rows, width), jnp.bfloat16)] * count,
        scratch_shapes=[
            pltpu.VMEM((count * rows, width), jnp.bfloat16),
            pltpu.VMEM((cuts, count * rows, step), jnp.bfloat16),
        ],
        compiler_params=pltpu.CompilerParams(vmem_limit_bytes=count * rows * width * 6 + (8 << 20)),
        cost_estimate=pl.CostEstimate(
            flops=count * rows * width * units * 6,
            bytes_accessed=count * rows * width * 4,
            transcendentals=count * rows * units,
        ),
        name="expert_part",
    )(*blocks, w_gate_up, w_down)


def combined(attended, weight, pieces):
    rows, width = attended.shape

    def body(*refs):
        att_ref, weight_ref = refs[:2]
        piece_refs, out_ref, x_ref = refs[2 : 2 + EXPERTS], refs[-2], refs[-1]
        for r in range(EXPERTS):
            x_ref[pl.ds(r * CAP, CAP), :] = piece_refs[r][...]
        weight = weight_ref[...]
        high = weight.astype(jnp.bfloat16)
        low = (weight - high.astype(jnp.float32)).astype(jnp.bfloat16)
        moe = jnp.dot(high, x_ref[...], preferred_element_type=jnp.float32)
        moe = moe + jnp.dot(low, x_ref[...], preferred_element_type=jnp.float32)
        out_ref[...] = (att_ref[...].astype(jnp.float32) + moe).astype(jnp.bfloat16)

    return pl.pallas_call(
        body,
        in_specs=[WHOLE] * (2 + EXPERTS),
        out_specs=WHOLE,
        out_shape=jax.ShapeDtypeStruct((rows, width), jnp.bfloat16),
        scratch_shapes=[pltpu.VMEM((EXPERTS * CAP, width), jnp.bfloat16)],
        compiler_params=pltpu.CompilerParams(vmem_limit_bytes=16 << 20),
        name="combined",
    )(attended, weight, *pieces)


def after(value, *events):
    return lax.optimization_barrier((value,) + events)[0]


def experts(slots, w_gate_up, w_down):
    def added(first, *others):
        total = first.astype(jnp.float32)
        for other in others:
            total = total + other.astype(jnp.float32)
        return total.astype(jnp.bfloat16)

    together = lax.optimization_barrier
    join = lambda *pieces: jnp.concatenate(pieces, axis=0)

    def part(mine, beside, before=(), behind=()):
        blocks = (mine, beside, swapped(mine, 1), swapped(beside, 1))
        if before:
            blocks = together((*blocks, *before))[:4]
        out = expert_part(blocks, w_gate_up, w_down)
        if behind:
            out = together((*out, *behind))[:4]
        return (out[0], swapped(out[2], 1)), added(out[1], swapped(out[3], 1))

    def home(rows, group):
        return [
            swapped(rows[at * CAP : (at + 1) * CAP], 4 * r) if r else rows[:CAP]
            for at, r in enumerate(group)
        ]

    z_1, x_0 = swapped(slots[1], 4), swapped(slots[0], 2)
    z_2, z_3 = swapped(slots[2], 8), swapped(slots[3], 12)
    z_4, z_5 = swapped(slots[4], 16), swapped(slots[5], 20)
    z_6 = swapped(after(slots[6], z_2, z_3), 24)
    z_7 = swapped(after(slots[7], z_2, z_3), 28)
    mine_a, mine_b = join(slots[0], z_1), join(z_2, z_3)
    beside_a, beside_b = join(x_0, swapped(z_1, 2)), swapped(mine_b, 2)
    own_a, sum_a = part(mine_a, beside_a)
    mine_c = join(after(z_4, own_a[0]), after(z_5, own_a[0]))
    beside_c = swapped(mine_c, 2)
    ret_a = swapped(sum_a, 2)
    own_b, sum_b = part(mine_b, beside_b, before=(sum_a,), behind=(beside_c,))
    mine_d = join(after(z_6, own_b[0]), after(z_7, own_b[0]))
    beside_d = swapped(mine_d, 2)
    own_c, sum_c = part(mine_c, beside_c, before=(sum_a, sum_b), behind=(beside_d, ret_a))
    ret_c = swapped(sum_c, 2)
    own_d, sum_d = part(mine_d, beside_d, before=(sum_c,), behind=(ret_c,))
    ret_d = swapped(sum_d, 2)
    home_a = home(added(*own_a, ret_a), (0, 1))
    home_c = home(added(*own_c, ret_c), (4, 5))
    ret_b = swapped(after(sum_b, ret_d), 2)
    home_d = home(added(*own_d, ret_d), (6, 7))
    home_b = home(added(*own_b, ret_b), (2, 3))
    return home_a + home_b + home_c + home_d


def per_device(
    residual,
    queries,
    new_kv,
    page_kv,
    page_node,
    leaf_parent,
    request_leaf,
    out_weight,
    router_weight,
    routes,
    w_gate_up,
    w_down,
):
    width = residual.shape[1]
    devices = lax.axis_size("dev")
    replicas = devices // BLOCK
    page_rows = page_kv.shape[0]
    gate_up_list = [w_gate_up]
    down_list = [w_down]
    for shift_step in range(1, replicas):
        arrived = passed_along((w_gate_up, w_down), "dev", BLOCK * shift_step)
        gate_up_list.append(arrived[0])
        down_list.append(arrived[1])
    if replicas > 1:
        w_gate_up = jnp.concatenate(gate_up_list, axis=1)
        w_down = jnp.concatenate(down_list, axis=0)
    me = lax.axis_index("dev")
    leaf_node = request_leaf[0]
    matches = jnp.arange(NL, dtype=jnp.int32) + NB + 1 == leaf_node
    branch_node = jnp.sum(jnp.where(matches, leaf_parent, 0))
    order = [c + y + x + z for c in (0, 1) for y in (0, 4) for x in (0, 2) for z in (0, 8, 16, 24)]
    order = [BLOCK * other + place for other in range(replicas) for place in order]
    owner = jnp.array(order, dtype=jnp.int32) ^ me
    owner = jnp.repeat(owner, page_rows)
    device_ids = jnp.arange(devices, dtype=jnp.int32)
    node_ids = jnp.sum(jnp.where(device_ids[:, None] == owner[None, :], page_node[:, None], 0), axis=0)
    visible = (node_ids == 0) | (node_ids == branch_node) | (node_ids == leaf_node)
    bias = jnp.where(visible, 0.0, masked_fill)[None, :]
    place_of = ((me % BLOCK) // 4).astype(jnp.int32).reshape(1)
    marks, picks = slot_tables(routes.T, place_of, out_weight)
    keys, values = gathered_pages(page_kv, width, replicas, bias, (marks, picks))
    attended, weight, *slots = front(
        queries, new_kv, keys, values, bias, residual, out_weight, router_weight.T, marks, picks
    )
    pieces = experts(slots, w_gate_up, w_down)
    return (attended, combined(attended, weight, pieces))


def solution(mesh):
    return jax.shard_map(
        per_device,
        mesh=mesh,
        in_specs=(
            P("dev", None),
            P("dev", None),
            P("dev", None),
            P("dev", None),
            P(),
            P(),
            P("dev"),
            P(),
            P(),
            P("dev", None),
            P(None, "dev", None),
            P("dev", None),
        ),
        out_specs=(P("dev", None), P("dev", None)),
        check_vma=False,
    )
```
